32 devices in a mesh: group: 2 (over x), tensor: 8 (over z, y), dp: 2 (over core).
Axes of the slice: x: 2, y: 2, z: 4, core: 2. Of those that a mesh axis runs over, the one named last changes fastest.
Arguments:
- tokens_in: bfloat16 [1536, 5120], P(('group', 'tensor', 'dp')), parts along dimension 0, may hold values from -6 to 6
- grad_out: bfloat16 [1536, 5120], P(('group', 'tensor', 'dp')), parts along dimension 0, may hold values from -6 to 6
- gate_blocks: bfloat16 [960, 128, 128], P('tensor'), may hold values from -0.15625 to 0.15625
- up_blocks: bfloat16 [960, 128, 128], P('tensor'), may hold values from -0.15625 to 0.15625
- down_blocks: bfloat16 [960, 128, 128], P('tensor'), may hold values from -0.109375 to 0.109375
- gate_index: int32 [960], P('tensor'), may hold values from 0 to 479, as said below
- up_index: int32 [960], P('tensor'), may hold values from 0 to 479, as said below
- down_index: int32 [960], P('tensor'), may hold values from 0 to 479, as said below
Outputs:
- output: bfloat16 [1536, 5120], P(('group', 'tensor', 'dp')), parts along dimension 0
- input_grad: bfloat16 [1536, 5120], P(('group', 'tensor', 'dp')), parts along dimension 0
- gate_grad_blocks: float32 [1920, 128, 128], P(('group', 'tensor', 'dp')), parts along dimension 0
- up_grad_blocks: float32 [1920, 128, 128], P(('group', 'tensor', 'dp')), parts along dimension 0
- down_grad_blocks: float32 [1920, 128, 128], P(('group', 'tensor', 'dp')), parts along dimension 0
The draws below stay inside these ranges and needn't reach their ends.
There are 2 independent parts, one for each index of `group`. The reference program is written for one: setup_inputs(seed, part) draws one part's arguments, and reference() takes and returns one part's arrays. A program takes and returns all parts, laid end to end along the dimension named above; an argument that names none is the same for every part. Nothing has to cross between parts.
Inputs may be any that keep to these rules, and one draw needn't show every extreme that they name: `gate_index`: each aligned run of 120 entries (the blocks of one tensor device) holds distinct values, among them 0 and 479. `up_index`: each aligned run of 120 entries (the blocks of one tensor device) holds distinct values, among them 0 and 479. `down_index`: each aligned run of 120 entries (the blocks of one tensor device) holds distinct values, among them 0 and 479.
All inputs are finite; a program needn't handle non-finite values.
Results may differ from the reference program's by a relative error of at most 0.0051.
Values may be sent and summed in bfloat16 or wider, within the bound.
No kernel may reach another device: no remote copies, remote signals or barrier semaphores. Data moves between devices by JAX's collectives and lax.ppermute only.
A program may use at most 320 MiB of HBM per device.

```python
import jax
import jax.numpy as jnp

D = 5120
FF = 12288
BLOCK = 128
TOKENS = 768
D_BLOCKS = 40
OWN_COLUMNS = 12
OWN_BLOCKS = 120
ALL_BLOCKS = 960
N_TENSOR = 8


def pick_blocks(key):
    slot_span = OWN_COLUMNS * D_BLOCKS
    owner_keys = jax.random.split(key, N_TENSOR)

    def one_owner(owner_key):
        first_key, second_key = jax.random.split(owner_key)
        interior = 1 + jax.random.permutation(first_key, slot_span - 2)[:OWN_BLOCKS - 2]
        chosen = jnp.concatenate([jnp.array([0, slot_span - 1], jnp.int32), interior.astype(jnp.int32)])
        return jax.random.permutation(second_key, chosen)
    return jax.vmap(one_owner)(owner_keys).reshape(-1).astype(jnp.int32)


def draw_gate_index(key, part):
    key = jax.random.fold_in(key, 3)
    return pick_blocks(key)


def draw_up_index(key, part):
    key = jax.random.fold_in(key, 5)
    return pick_blocks(key)


def draw_down_index(key, part):
    key = jax.random.fold_in(key, 7)
    return pick_blocks(key)


def shard_levels(stream_key, shape, cuts, low, high):
    def one(position, shards_of):
        steps = jax.random.uniform(jax.random.fold_in(jax.random.fold_in(stream_key, 6), position), (shards_of,), jnp.float32, low / len(cuts), high / len(cuts))
        return jnp.repeat(jnp.exp(steps), shape[position] // shards_of).reshape((-1,) + (1,) * (len(shape) - position - 1))

    gain = one(*cuts[0])
    for cut in cuts[1:]:
        gain = gain * one(*cut)
    return gain


def scatter_about(rng, extent, scale, reach, cuts=(), held_as=jnp.bfloat16):
    entries = jax.random.normal(rng, extent, jnp.float32) * scale
    if len(cuts) > 0:
        entries = shard_levels(rng, extent, cuts, -0.22, 0.18) * entries
    return jnp.clip(entries, min=-reach, max=reach).astype(held_as)


def setup_inputs(seed: int = 0, part: int = 0) -> dict:
    splits = jax.random.split(jax.random.key(seed), 9)
    part_keys = jax.random.split(jax.random.fold_in(splits[8], part), 9)
    tokens_in = scatter_about(part_keys[0], (TOKENS, D), 1.0, 6.0, ((0, 16),))
    grad_out = scatter_about(part_keys[1], (TOKENS, D), 1.0, 6.0, ((0, 16),))
    gate_blocks = scatter_about(splits[2], (ALL_BLOCKS, BLOCK, BLOCK), (D // 4) ** -0.5, 0.15625, ((0, 8),))
    up_blocks = scatter_about(splits[3], (ALL_BLOCKS, BLOCK, BLOCK), (D // 4) ** -0.5, 0.15625, ((0, 8),))
    down_blocks = scatter_about(splits[4], (ALL_BLOCKS, BLOCK, BLOCK), (FF // 4) ** -0.5, 0.109375, ((0, 8),))
    gate_index = draw_gate_index(jax.random.fold_in(splits[8], 71), part)
    up_index = draw_up_index(jax.random.fold_in(splits[8], 71), part)
    down_index = draw_down_index(jax.random.fold_in(splits[8], 71), part)
    return {"tokens_in": tokens_in, "grad_out": grad_out, "gate_blocks": gate_blocks, "up_blocks": up_blocks, "down_blocks": down_blocks, "gate_index": gate_index, "up_index": up_index, "down_index": down_index}


def owner_columns(block_index):
    owner_ids = (jnp.arange(ALL_BLOCKS) // OWN_BLOCKS).astype(jnp.int32)
    row_block = (block_index % D_BLOCKS).astype(jnp.int32)
    col_block = (owner_ids * OWN_COLUMNS + block_index // D_BLOCKS).astype(jnp.int32)
    return (row_block, col_block)

def spread_in(blocks, block_index):
    row_block, col_block = owner_columns(block_index)
    f_blocks = FF // BLOCK
    tiled = jnp.zeros((D_BLOCKS, f_blocks, BLOCK, BLOCK), blocks.dtype).at[row_block, col_block].set(blocks)
    return tiled.transpose(0, 2, 1, 3).reshape(D, FF)

def spread_out(blocks, block_index):
    row_block, col_block = owner_columns(block_index)
    f_blocks = FF // BLOCK
    tiled = jnp.zeros((f_blocks, D_BLOCKS, BLOCK, BLOCK), blocks.dtype).at[col_block, row_block].set(blocks)
    return tiled.transpose(0, 2, 1, 3).reshape(FF, D)

def pick_in(dense, block_index):
    row_block, col_block = owner_columns(block_index)
    return dense.reshape(D_BLOCKS, BLOCK, FF // BLOCK, BLOCK)[row_block, :, col_block, :]

def pick_out(dense, block_index):
    row_block, col_block = owner_columns(block_index)
    return dense.reshape(FF // BLOCK, BLOCK, D_BLOCKS, BLOCK)[col_block, :, row_block, :]

def reference(tokens_in, grad_out, gate_blocks, up_blocks, down_blocks, gate_index, up_index, down_index):
    gate_dense = spread_in(gate_blocks, gate_index)
    up_dense = spread_in(up_blocks, up_index)
    down_dense = spread_out(down_blocks, down_index)
    gate_pre = jnp.dot(tokens_in, gate_dense, preferred_element_type=jnp.float32)
    up_pre = jnp.dot(tokens_in, up_dense, preferred_element_type=jnp.float32)
    sigmoid_vals = jax.nn.sigmoid(gate_pre)
    activated = gate_pre * sigmoid_vals
    hidden = (activated * up_pre).astype(jnp.bfloat16)
    output = jnp.dot(hidden, down_dense, preferred_element_type=jnp.float32).astype(jnp.bfloat16)
    hidden_grad = jnp.dot(grad_out, down_dense.T, preferred_element_type=jnp.float32)
    gate_grad = (hidden_grad * up_pre * sigmoid_vals * (1.0 + gate_pre * (1.0 - sigmoid_vals))).astype(jnp.bfloat16)
    up_grad = (hidden_grad * activated).astype(jnp.bfloat16)
    input_grad = (jnp.dot(gate_grad, gate_dense.T, preferred_element_type=jnp.float32) + jnp.dot(up_grad, up_dense.T, preferred_element_type=jnp.float32)).astype(jnp.bfloat16)
    grad_scale = jnp.float32(1.0) / jnp.sqrt(jnp.float32(TOKENS))
    gate_grad_blocks = pick_in(jnp.dot(tokens_in.T, gate_grad, preferred_element_type=jnp.float32), gate_index) * grad_scale
    up_grad_blocks = pick_in(jnp.dot(tokens_in.T, up_grad, preferred_element_type=jnp.float32), up_index) * grad_scale
    down_grad_blocks = pick_out(jnp.dot(hidden.T, grad_out, preferred_element_type=jnp.float32), down_index) * grad_scale
    return (output, input_grad, gate_grad_blocks, up_grad_blocks, down_grad_blocks)
```

```python
import functools

import jax
import jax.numpy as jnp
from jax import lax
from jax.experimental import pallas as pl
from jax.experimental.pallas import tpu as pltpu
from jax.sharding import PartitionSpec as P

FF = 12288
VMEM_LIMIT = 40 * 2**20
PARTS_IN = 3
PARTS_OUT = 2

SMEM_SPEC = pl.BlockSpec(memory_space=pltpu.SMEM)
VMEM_SPEC = pl.BlockSpec(memory_space=pltpu.VMEM)
ANY_SPEC = pl.BlockSpec(memory_space=pl.ANY)


def ring_order(size):
    return list(range(0, size, 2)) + list(range(1, size, 2))[::-1]


def ring_shifts(size):
    order = ring_order(size)
    ahead = [(order[i], order[(i + 1) % size]) for i in range(size)]
    back = [(b, a) for a, b in ahead]

    def to_right(value):
        return lax.ppermute(value, "tensor", ahead)

    def to_left(value):
        return lax.ppermute(value, "tensor", back)

    return to_right, to_left


def ring_gather(rows, size):
    to_right, to_left = ring_shifts(size)
    half = rows.shape[0] // 2
    blocks = [rows]
    from_left = from_right = rows
    for _ in range(size // 2 - 1):
        from_left, from_right = to_right(from_left), to_left(from_right)
        blocks += [from_left, from_right]
    blocks += [to_right(from_left[:half]), to_left(from_right[half:])]
    return jnp.concatenate(blocks, axis=0)


def ring_scatter(parts, size):
    to_right, to_left = ring_shifts(size)
    rows = parts.shape[0] // size
    half = rows // 2
    far = size // 2

    def block(place):
        return parts[place * rows:(place + 1) * rows]

    right = block(size - 1)[:half].astype(jnp.bfloat16)
    left = block(size - 1)[half:].astype(jnp.bfloat16)
    for distance in range(far - 1, -1, -1):
        right, left = to_right(right), to_left(left)
        if distance == 0:
            break
        toward_right, toward_left = block(2 * distance), block(2 * distance - 1)
        if distance == far - 1:
            right = jnp.concatenate(
                [right.astype(jnp.float32) + toward_right[:half], toward_right[half:]], axis=0
            )
            left = jnp.concatenate(
                [toward_left[:half], left.astype(jnp.float32) + toward_left[half:]], axis=0
            )
        else:
            right = right.astype(jnp.float32) + toward_right
            left = left.astype(jnp.float32) + toward_left
        right, left = right.astype(jnp.bfloat16), left.astype(jnp.bfloat16)
    return (block(0) + right.astype(jnp.float32) + left.astype(jnp.float32)).astype(jnp.bfloat16)


def slot_table(index, slots):
    count = index.shape[0]
    hit = index[None, :] == jnp.arange(slots, dtype=jnp.int32)[:, None]
    return jnp.min(jnp.where(hit, jnp.arange(count, dtype=jnp.int32)[None, :], count), axis=1)


def with_zero(blocks):
    return jnp.concatenate([blocks, jnp.zeros((1,) + blocks.shape[1:], blocks.dtype)], axis=0)


def columns_of(lhs, weights, place, first, depth, b):
    strip = jnp.concatenate(
        [
            jnp.concatenate([weights[place(first + n, m)] for n in range(2)], axis=1)
            for m in range(depth)
        ],
        axis=0,
    )
    return jnp.dot(lhs, strip, preferred_element_type=jnp.float32)


def columns_of_turned(lhs, weights, place, first, depth, b):
    strip = jnp.concatenate(
        [
            jnp.concatenate([weights[place(first + n, m)] for m in range(depth)], axis=1)
            for n in range(2)
        ],
        axis=0,
    )
    return lax.dot_general(
        lhs, strip, (((1,), (1,)), ((), ())), preferred_element_type=jnp.float32
    )


def hidden_kernel(dim_blocks, offset, gate_at, up_at, x, gate_w, up_w, *rest):
    hidden, act, slope = rest[-3:]
    first = (offset + pl.program_id(0)) * 2
    b = gate_w.shape[1]

    def strip(at, w):
        return columns_of(
            x[...], w, lambda n, m: at[n * dim_blocks + m], first, dim_blocks, b
        )

    gate = strip(gate_at, gate_w)
    up = strip(up_at, up_w)
    sig = jax.nn.sigmoid(gate)
    activated = gate * sig
    hidden[...] = (activated * up).astype(jnp.bfloat16)
    act[...] = activated
    slope[...] = up * sig * (1.0 + gate * (1.0 - sig))


def grads_kernel(dim_blocks, offset, down_at, g, down_w, act, slope, *rest):
    gate_grad, up_grad = rest[-2:]
    first = (offset + pl.program_id(0)) * 2
    b = down_w.shape[1]
    hidden_grad = columns_of_turned(
        g[...], down_w, lambda n, m: down_at[n * dim_blocks + m], first, dim_blocks, b
    )
    gate_grad[...] = (hidden_grad * slope[...]).astype(jnp.bfloat16)
    up_grad[...] = (hidden_grad * act[...]).astype(jnp.bfloat16)


def output_kernel(dim_blocks, columns, offset, down_at, hidden, down_w, *rest):
    out = rest[-1]
    first = (offset + pl.program_id(0)) * 2
    out[...] = columns_of(
        hidden[...], down_w, lambda n, m: down_at[m * dim_blocks + n], first, columns,
        down_w.shape[1],
    )


def input_grad_kernel(
    dim_blocks, columns, offset, gate_at, up_at, gate_grad, up_grad, gate_w, up_w, *rest
):
    out = rest[-1]
    first = (offset + pl.program_id(0)) * 2
    b = gate_w.shape[1]

    def strip(lhs, at, w):
        return columns_of_turned(
            lhs[...], w, lambda n, m: at[m * dim_blocks + n], first, columns, b
        )

    out[...] = strip(gate_grad, gate_at, gate_w) + strip(up_grad, up_at, up_w)


def strips(kernel, inputs, specs, outs, offset, count, block_outs, flops):
    rows = block_outs[0].shape[0]
    width = 2 * 128

    def strip_spec():
        return pl.BlockSpec((rows, width), lambda i: (0, offset + i))

    in_specs = [strip_spec() if spec is None else spec for spec in specs]
    aliases = {}
    if outs is not None:
        aliases = {len(inputs) + i: i for i in range(len(outs))}
        inputs = list(inputs) + list(outs)
        in_specs += [ANY_SPEC] * len(outs)
    return pl.pallas_call(
        functools.partial(kernel, offset),
        grid=(count,),
        in_specs=in_specs,
        out_specs=[strip_spec() for _ in block_outs],
        out_shape=list(block_outs),
        input_output_aliases=aliases,
        compiler_params=pltpu.CompilerParams(vmem_limit_bytes=VMEM_LIMIT),
        cost_estimate=pl.CostEstimate(flops=flops, bytes_accessed=8 * 2**20, transcendentals=0),
    )(*inputs)


def in_calls(kernel, inputs, specs, total, calls, block_outs, flops):
    outs = None
    calls = calls if total % calls == 0 else 1
    for call in range(calls):
        count = total // calls
        outs = strips(
            kernel, inputs, specs, outs, call * count, count, block_outs, flops // calls
        )
    return outs


def block_grads(left, right, index, dim_blocks, left_is_model, arrived, scale):
    count = index.shape[0]
    rows = left.shape[0]
    b = 128
    group = max(d for d in range(1, 13) if count % d == 0)

    def kernel(at, left_ref, right_ref, *rest):
        out = rest[-1]
        base = pl.program_id(0) * group
        for i in range(group):
            slot = at[base + i]
            model, hidden = slot % dim_blocks, slot // dim_blocks
            a, c = (model, hidden) if left_is_model else (hidden, model)
            value = lax.dot_general(
                left_ref[:, pl.ds(pl.multiple_of(a * b, b), b)],
                right_ref[:, pl.ds(pl.multiple_of(c * b, b), b)],
                (((0,), (0,)), ((), ())),
                preferred_element_type=jnp.float32,
            )
            if arrived is not None:
                value = (value + rest[0][i].astype(jnp.float32)) * scale
            out[i] = value.astype(out.dtype)

    spec = pl.BlockSpec((group, b, b), lambda i: (i, 0, 0))
    extra = [] if arrived is None else [arrived]
    dtype = jnp.bfloat16 if arrived is None else jnp.float32
    return pl.pallas_call(
        kernel,
        grid=(count // group,),
        in_specs=[SMEM_SPEC, VMEM_SPEC, VMEM_SPEC] + [spec] * len(extra),
        out_specs=spec,
        out_shape=jax.ShapeDtypeStruct((count, b, b), dtype),
        compiler_params=pltpu.CompilerParams(vmem_limit_bytes=VMEM_LIMIT),
        cost_estimate=pl.CostEstimate(
            flops=8 * count * rows * b * b, bytes_accessed=8 * 2**20, transcendentals=0
        ),
    )(index, left, right, *extra)


def body(
    tokens_in, grad_out, gate_blocks, up_blocks, down_blocks, gate_index, up_index, down_index
):
    block_size = gate_blocks.shape[1]
    model_width = tokens_in.shape[1]
    dim_blocks = model_width // block_size
    owners = lax.axis_size("tensor")
    columns = FF // (block_size * owners)
    width = columns * block_size
    token_count = tokens_in.shape[0] * owners
    count = gate_blocks.shape[0]
    slots = columns * dim_blocks

    gate_at, up_at, down_at = (slot_table(i, slots) for i in (gate_index, up_index, down_index))
    gate_w, up_w, down_w = (with_zero(w) for w in (gate_blocks, up_blocks, down_blocks))

    x = ring_gather(tokens_in, owners)
    g = ring_gather(grad_out, owners)

    unit = 2 * token_count * model_width * width
    narrow = jax.ShapeDtypeStruct((token_count, width), jnp.bfloat16)
    wide = jax.ShapeDtypeStruct((token_count, width), jnp.float32)
    total = jax.ShapeDtypeStruct((token_count, model_width), jnp.float32)

    hidden, act, slope = in_calls(
        functools.partial(hidden_kernel, dim_blocks),
        [gate_at, up_at, x, gate_w, up_w],
        [SMEM_SPEC] * 2 + [VMEM_SPEC] * 3,
        columns // 2, PARTS_IN, [narrow, wide, wide], 2 * unit,
    )
    (out_parts,) = in_calls(
        functools.partial(output_kernel, dim_blocks, columns),
        [down_at, hidden, down_w],
        [SMEM_SPEC] + [VMEM_SPEC] * 2,
        dim_blocks // 2, PARTS_OUT, [total], unit,
    )
    output = ring_scatter(out_parts, owners)

    gate_grad, up_grad = in_calls(
        functools.partial(grads_kernel, dim_blocks),
        [down_at, g, down_w, act, slope],
        [SMEM_SPEC] + [VMEM_SPEC] * 2 + [None] * 2,
        columns // 2, PARTS_IN, [narrow, narrow], unit,
    )
    (grad_parts,) = in_calls(
        functools.partial(input_grad_kernel, dim_blocks, columns),
        [gate_at, up_at, gate_grad, up_grad, gate_w, up_w],
        [SMEM_SPEC] * 2 + [VMEM_SPEC] * 4,
        dim_blocks // 2, PARTS_OUT, [total], 2 * unit,
    )
    input_grad = ring_scatter(grad_parts, owners)

    pairs = lax.axis_size("dp")
    share = count // pairs
    me = lax.axis_index("dp")
    scale = 1.0 / float(token_count * pairs) ** 0.5
    swap = [(0, 1), (1, 0)]
    sums = []
    for left, right, index, left_is_model in (
        (hidden, g, down_index, False),
        (x, gate_grad, gate_index, True),
        (x, up_grad, up_index, True),
    ):
        theirs = lax.dynamic_slice(index, ((1 - me) * share,), (share,))
        mine = lax.dynamic_slice(index, (me * share,), (share,))
        sent = block_grads(left, right, theirs, dim_blocks, left_is_model, None, None)
        arrived = lax.ppermute(sent, "dp", swap)
        sums.append(block_grads(left, right, mine, dim_blocks, left_is_model, arrived, scale))
    return output, input_grad, sums[1], sums[2], sums[0]


def solution(mesh):
    rows = P(("group", "tensor", "dp"), None)
    owned = P("tensor", None, None)
    grads = P(("group", "tensor", "dp"), None, None)
    return jax.shard_map(
        body,
        mesh=mesh,
        in_specs=(rows, rows, owned, owned, owned, P("tensor"), P("tensor"), P("tensor")),
        out_specs=(rows, rows, grads, grads, grads),
        check_vma=False,
    )
```

```python
import functools

import jax
import jax.numpy as jnp
from jax import lax
from jax.experimental import pallas as pl
from jax.experimental.pallas import tpu as pltpu
from jax.sharding import PartitionSpec as P

FF = 12288

SMEM_SPEC = pl.BlockSpec(memory_space=pltpu.SMEM)
WHOLE = "whole"
ANY_SPEC = pl.BlockSpec(memory_space=pl.ANY)


def ring_order(size):
    return list(range(0, size, 2)) + list(range(1, size, 2))[::-1]


def ring_shifts(size):
    order = ring_order(size)
    ahead = [(order[i], order[(i + 1) % size]) for i in range(size)]
    back = [(b, a) for a, b in ahead]

    def to_right(value):
        return lax.ppermute(value, "tensor", ahead)

    def to_left(value):
        return lax.ppermute(value, "tensor", back)

    return to_right, to_left


def after_all(values, events):
    values = tuple(values)
    return lax.optimization_barrier(values + tuple(events))[:len(values)] if events else values


class Gather:
    def __init__(self, rows, size):
        self.to_right, self.to_left = ring_shifts(size)
        self.half = rows.shape[0] // 2
        self.last = size // 2 - 1
        self.blocks = [rows]
        self.from_left = self.from_right = rows
        self.taken = 0

    def step(self, events=()):
        left, right = after_all((self.from_left, self.from_right), events)
        if self.taken == self.last:
            left, right = left[:self.half], right[self.half:]
        self.from_left, self.from_right = self.to_right(left), self.to_left(right)
        self.blocks += [self.from_left, self.from_right]
        self.taken += 1
        return self.from_left, self.from_right

    def result(self, events=()):
        return jnp.concatenate(after_all(self.blocks, events), axis=0)


class Scatter:
    def __init__(self, near, far, size):
        self.to_right, self.to_left = ring_shifts(size)
        self.near = near
        self.rows = far.shape[0]
        self.half = self.rows // 2
        self.distance = size // 2
        self.right, self.left = far[:self.half], far[self.half:]

    def block(self, place):
        return self.near[place * self.rows:(place + 1) * self.rows]

    def step(self, events=()):
        right, left = after_all((self.right, self.left), events)
        right, left = self.to_right(right), self.to_left(left)
        self.distance -= 1
        self.right, self.left = right, left
        if self.distance > 0:
            if right.shape[0] == self.half:
                none = jnp.zeros_like(right)
                right = jnp.concatenate([right, none], axis=0)
                left = jnp.concatenate([none, left], axis=0)
            right = right.astype(jnp.float32) + self.block(2 * self.distance)
            left = left.astype(jnp.float32) + self.block(2 * self.distance - 1)
            self.right, self.left = right.astype(jnp.bfloat16), left.astype(jnp.bfloat16)
        return self.right, self.left

    def result(self):
        total = self.block(0) + self.right.astype(jnp.float32) + self.left.astype(jnp.float32)
        return total.astype(jnp.bfloat16)


def slot_table(index, slots):
    count = index.shape[0]
    hit = index[None, :] == jnp.arange(slots, dtype=jnp.int32)[:, None]
    return jnp.min(jnp.where(hit, jnp.arange(count, dtype=jnp.int32)[None, :], count), axis=1)


def with_zero(blocks):
    return jnp.concatenate([blocks, jnp.zeros((1,) + blocks.shape[1:], blocks.dtype)], axis=0)


def columns_of(lhs, weights, place, first, depth, b):
    strip = jnp.concatenate(
        [
            jnp.concatenate([weights[place(first + n, m)] for n in range(2)], axis=1)
            for m in range(depth)
        ],
        axis=0,
    )
    return jnp.dot(lhs, strip, preferred_element_type=jnp.float32)


def columns_of_turned(lhs, weights, place, first, depth, b):
    strip = jnp.concatenate(
        [
            jnp.concatenate([weights[place(first + n, m)] for m in range(depth)], axis=1)
            for n in range(2)
        ],
        axis=0,
    )
    return lax.dot_general(
        lhs, strip, (((1,), (1,)), ((), ())), preferred_element_type=jnp.float32
    )


def hidden_kernel(dim_blocks, offset, gate_at, up_at, x, gate_w, up_w, *rest):
    hidden, act, slope = rest[-4:-1]
    first = (offset + pl.program_id(0)) * 2
    b = gate_w.shape[1]

    def strip(at, w):
        return columns_of(
            x[...], w, lambda n, m: at[n * dim_blocks + m], first, dim_blocks, b
        )

    gate = strip(gate_at, gate_w)
    up = strip(up_at, up_w)
    sig = jax.nn.sigmoid(gate)
    activated = gate * sig
    hidden[...] = (activated * up).astype(jnp.bfloat16)
    act[...] = activated
    slope[...] = up * sig * (1.0 + gate * (1.0 - sig))


def grads_kernel(dim_blocks, offset, down_at, g, down_w, act, slope, *rest):
    gate_grad, up_grad = rest[-3:-1]
    first = (offset + pl.program_id(0)) * 2
    b = down_w.shape[1]
    hidden_grad = columns_of_turned(
        g[...], down_w, lambda n, m: down_at[n * dim_blocks + m], first, dim_blocks, b
    )
    gate_grad[...] = (hidden_grad * slope[...]).astype(jnp.bfloat16)
    up_grad[...] = (hidden_grad * act[...]).astype(jnp.bfloat16)


def split_rows(value, near, far):
    rows = near.shape[0]
    near[...] = value[:rows]
    far[...] = value[rows:].astype(far.dtype)


def output_kernel(dim_blocks, columns, offset, down_at, hidden, down_w, *rest):
    first = (offset + pl.program_id(0)) * 2
    split_rows(
        columns_of(
            hidden[...], down_w, lambda n, m: down_at[m * dim_blocks + n], first, columns,
            down_w.shape[1],
        ),
        *rest[-3:-1],
    )


def input_grad_kernel(
    dim_blocks, columns, offset, gate_at, up_at, gate_grad, up_grad, gate_w, up_w, *rest
):
    first = (offset + pl.program_id(0)) * 2
    b = gate_w.shape[1]

    def strip(lhs, at, w):
        return columns_of_turned(
            lhs[...], w, lambda n, m: at[m * dim_blocks + n], first, columns, b
        )

    split_rows(
        strip(gate_grad, gate_at, gate_w) + strip(up_grad, up_at, up_w), *rest[-3:-1]
    )


def whole_spec(array):
    zeros = (0,) * len(array.shape)
    return pl.BlockSpec(array.shape, lambda i: zeros, pipeline_mode=pl.Buffered(1))


def room(arrays, spare):
    held = sum(a.dtype.itemsize * a.size for a in arrays)
    return pltpu.CompilerParams(vmem_limit_bytes=held + spare * 2**20)


class Strips:
    def __init__(self, kernel, inputs, specs, total, block_outs, flops):
        self.kernel, self.inputs, self.specs = kernel, inputs, specs
        self.total, self.block_outs, self.flops = total, block_outs, flops
        self.outs = []
        self.done = 0

    def run(self, share, events=()):
        offset = self.done
        count = round(self.total * share) - offset
        self.done += count

        def strip_spec(array):
            return pl.BlockSpec((array.shape[0], 2 * 128), lambda i: (0, offset + i))

        inputs = [*after_all(self.inputs[:1], events), *self.inputs[1:], *self.outs]
        in_specs = [
            strip_spec(array) if spec is None else whole_spec(array) if spec is WHOLE else spec
            for array, spec in zip(inputs, self.specs)
        ] + [ANY_SPEC] * len(self.outs)
        first_out = len(self.inputs)

        def kernel(*refs):
            self.kernel(offset, *refs)
            refs[-1][...] = jnp.zeros_like(refs[-1])

        *outs, token = pl.pallas_call(
            kernel,
            grid=(count,),
            in_specs=in_specs,
            out_specs=[strip_spec(out) for out in self.block_outs]
            + [pl.BlockSpec((8, 128), lambda i: (0, 0))],
            out_shape=list(self.block_outs) + [jax.ShapeDtypeStruct((8, 128), jnp.int32)],
            input_output_aliases={first_out + i: i for i in range(len(self.outs))},
            compiler_params=room(
                [array for array, spec in zip(inputs, self.specs) if spec is WHOLE], 12
            ),
            cost_estimate=pl.CostEstimate(
                flops=2 * self.flops * count // self.total, bytes_accessed=8 * 2**20,
                transcendentals=0,
            ),
        )(*inputs)
        self.outs = outs
        return (token,)


def block_grads(left, right, index, dim_blocks, left_is_model, arrived, scale):
    count = index.shape[0]
    rows = left.shape[0]
    b = 128
    group = max(d for d in range(1, 13) if count % d == 0)

    def kernel(at, left_ref, right_ref, *rest):
        out = rest[-1]
        base = pl.program_id(0) * group
        for i in range(group):
            slot = at[base + i]
            model, hidden = slot % dim_blocks, slot // dim_blocks
            a, c = (model, hidden) if left_is_model else (hidden, model)
            value = lax.dot_general(
                left_ref[:, pl.ds(pl.multiple_of(a * b, b), b)],
                right_ref[:, pl.ds(pl.multiple_of(c * b, b), b)],
                (((0,), (0,)), ((), ())),
                preferred_element_type=jnp.float32,
            )
            if arrived is not None:
                value = (value + rest[0][i].astype(jnp.float32)) * scale
            out[i] = value.astype(out.dtype)

    spec = pl.BlockSpec((group, b, b), lambda i: (i, 0, 0))
    extra = [] if arrived is None else [arrived]
    dtype = jnp.bfloat16 if arrived is None else jnp.float32
    return pl.pallas_call(
        kernel,
        grid=(count // group,),
        in_specs=[SMEM_SPEC, whole_spec(left), whole_spec(right)] + [spec] * len(extra),
        out_specs=spec,
        out_shape=jax.ShapeDtypeStruct((count, b, b), dtype),
        compiler_params=room([left, right], 10),
        cost_estimate=pl.CostEstimate(
            flops=8 * count * rows * b * b, bytes_accessed=8 * 2**20, transcendentals=0
        ),
    )(index, left, right, *extra)


def body(
    tokens_in, grad_out, gate_blocks, up_blocks, down_blocks, gate_index, up_index, down_index
):
    block_size = gate_blocks.shape[1]
    model_width = tokens_in.shape[1]
    dim_blocks = model_width // block_size
    owners = lax.axis_size("tensor")
    columns = FF // (block_size * owners)
    width = columns * block_size
    token_count = tokens_in.shape[0] * owners
    count = gate_blocks.shape[0]
    slots = columns * dim_blocks

    steps = owners // 2
    unit = 2 * token_count * model_width * width
    narrow = jax.ShapeDtypeStruct((token_count, width), jnp.bfloat16)
    wide = jax.ShapeDtypeStruct((token_count, width), jnp.float32)
    held_rows = tokens_in.shape[0]
    totals = [
        jax.ShapeDtypeStruct((token_count - held_rows, model_width), jnp.float32),
        jax.ShapeDtypeStruct((held_rows, model_width), jnp.bfloat16),
    ]

    assert steps % 4 == 0

    def several(chain, quarters, events=()):
        for _ in range(steps * quarters // 4):
            events = chain.step(events)
        return tuple(events)

    x_ring, g_ring = Gather(tokens_in, owners), Gather(grad_out, owners)
    events = several(x_ring, 1)
    gate_at, up_at = slot_table(gate_index, slots), slot_table(up_index, slots)
    gate_w = with_zero(gate_blocks)
    events = several(x_ring, 1, events + (gate_at, up_at, gate_w[-1, :8]))
    up_w = with_zero(up_blocks)
    events = several(x_ring, 1, events + (up_w[-1, :8],))
    down_at, down_w = slot_table(down_index, slots), with_zero(down_blocks)
    events = several(x_ring, 1, events + (down_at, down_w[-1, :8]))
    x = x_ring.result()

    hidden_strips = Strips(
        functools.partial(hidden_kernel, dim_blocks),
        [gate_at, up_at, x, gate_w, up_w],
        [SMEM_SPEC] * 2 + [WHOLE] * 3,
        columns // 2, [narrow, wide, wide], 2 * unit,
    )
    events = several(g_ring, 1, events) + hidden_strips.run(0.5, events)
    events = several(g_ring, 1, events) + hidden_strips.run(1, events)
    hidden, act, slope = hidden_strips.outs
    out_strips = Strips(
        functools.partial(output_kernel, dim_blocks, columns),
        [down_at, hidden, down_w],
        [SMEM_SPEC] + [WHOLE] * 2,
        dim_blocks // 2, totals, unit,
    )
    events = several(g_ring, 1, events) + out_strips.run(1, events)
    out_ring = Scatter(*out_strips.outs, owners)
    events = several(g_ring, 1, events) + several(out_ring, 1)
    g = g_ring.result(events)

    grads_strips = Strips(
        functools.partial(grads_kernel, dim_blocks),
        [down_at, g, down_w, act, slope],
        [SMEM_SPEC] + [WHOLE] * 2 + [None] * 2,
        columns // 2, [narrow, narrow], unit,
    )
    events = several(out_ring, 1, events) + grads_strips.run(1, events)
    gate_grad, up_grad = grads_strips.outs
    in_strips = Strips(
        functools.partial(input_grad_kernel, dim_blocks, columns),
        [gate_at, up_at, gate_grad, up_grad, gate_w, up_w],
        [SMEM_SPEC] * 2 + [WHOLE] * 4,
        dim_blocks // 2, totals, 2 * unit,
    )
    events = several(out_ring, 1, events) + in_strips.run(0.5, events)
    events = several(out_ring, 1, events) + in_strips.run(1, events)
    output = out_ring.result()

    in_ring = Scatter(*in_strips.outs, owners)
    pairs = lax.axis_size("dp")
    share = count // pairs
    me = lax.axis_index("dp")
    scale = 1.0 / float(token_count * pairs) ** 0.5
    work = (
        (hidden, g, down_index, False),
        (x, gate_grad, gate_index, True),
        (x, up_grad, up_index, True),
    )

    def theirs(i, events):
        left, right, index, left_is_model = work[i]
        (held,) = after_all([lax.dynamic_slice(index, ((1 - me) * share,), (share,))], events)
        return block_grads(left, right, held, dim_blocks, left_is_model, None, None)

    def mine(i, arrived, events):
        left, right, index, left_is_model = work[i]
        (held,) = after_all([lax.dynamic_slice(index, (me * share,), (share,))], events)
        return block_grads(left, right, held, dim_blocks, left_is_model, arrived, scale)

    def swap(sent):
        return lax.ppermute(sent, "dp", [(0, 1), (1, 0)])

    sent_down = theirs(0, events)
    events = several(in_ring, 1, events) + (sent_down,)
    down_arrived = swap(sent_down)
    sent = [theirs(1, events), theirs(2, events)]
    events = several(in_ring, 1, events) + (*sent, down_arrived)
    gate_arrived, up_arrived = swap(sent[0]), swap(sent[1])
    down_sum = mine(0, down_arrived, events)
    events = several(in_ring, 1, events) + (down_sum[:1, :8], gate_arrived, up_arrived)
    gate_sum = mine(1, gate_arrived, events)
    up_sum = mine(2, up_arrived, events)
    several(in_ring, 1, events)
    input_grad = in_ring.result()
    return output, input_grad, gate_sum, up_sum, down_sum


def solution(mesh):
    rows = P(("group", "tensor", "dp"), None)
    owned = P("tensor", None, None)
    grads = P(("group", "tensor", "dp"), None, None)
    return jax.shard_map(
        body,
        mesh=mesh,
        in_specs=(rows, rows, owned, owned, owned, P("tensor"), P("tensor"), P("tensor")),
        out_specs=(rows, rows, grads, grads, grads),
        check_vma=False,
    )
```

```python
import functools

import jax
import jax.numpy as jnp
from jax import lax
from jax.experimental import pallas as pl
from jax.experimental.pallas import tpu as pltpu
from jax.sharding import PartitionSpec as P

FF = 12288

SMEM_SPEC = pl.BlockSpec(memory_space=pltpu.SMEM)
WHOLE = "whole"
ANY_SPEC = pl.BlockSpec(memory_space=pl.ANY)


def ring_order(size):
    return list(range(0, size, 2)) + list(range(1, size, 2))[::-1]


def ring_shifts(size):
    order = ring_order(size)
    ahead = [(order[i], order[(i + 1) % size]) for i in range(size)]
    back = [(b, a) for a, b in ahead]

    def to_right(value):
        return lax.ppermute(value, "tensor", ahead)

    def to_left(value):
        return lax.ppermute(value, "tensor", back)

    return to_right, to_left


def after_all(values, events):
    values = tuple(values)
    return lax.optimization_barrier(values + tuple(events))[:len(values)] if events else values


class Gather:
    def __init__(self, rows, size):
        self.to_right, self.to_left = ring_shifts(size)
        self.half = rows.shape[0] // 2
        self.last = size // 2 - 1
        self.blocks = [rows]
        self.from_left = self.from_right = rows
        self.taken = 0

    def step(self, events=()):
        left, right = after_all((self.from_left, self.from_right), events)
        if self.taken == self.last:
            left, right = left[:self.half], right[self.half:]
        self.from_left, self.from_right = self.to_right(left), self.to_left(right)
        self.blocks += [self.from_left, self.from_right]
        self.taken += 1
        return self.from_left, self.from_right

    def first_rows(self, events):
        return jnp.concatenate(after_all(self.blocks[:self.last + 1], events), axis=0)

    def all_rows(self, events):
        return jnp.concatenate(after_all(self.blocks, events), axis=0)

    def last_rows(self, events):
        return jnp.concatenate(after_all(self.blocks[self.last + 1:], events), axis=0)


class Scatter:
    def __init__(self, near, far, size):
        self.to_right, self.to_left = ring_shifts(size)
        self.near = near
        self.rows = far.shape[0]
        self.half = self.rows // 2
        self.distance = size // 2
        self.right, self.left = far[:self.half], far[self.half:]

    def block(self, place):
        return self.near[place * self.rows:(place + 1) * self.rows]

    def step(self, events=()):
        right, left = after_all((self.right, self.left), events)
        right, left = self.to_right(right), self.to_left(left)
        self.distance -= 1
        self.right, self.left = right, left
        if self.distance > 0:
            if right.shape[0] == self.half:
                none = jnp.zeros_like(right)
                right = jnp.concatenate([right, none], axis=0)
                left = jnp.concatenate([none, left], axis=0)
            right = right.astype(jnp.float32) + self.block(2 * self.distance)
            left = left.astype(jnp.float32) + self.block(2 * self.distance - 1)
            self.right, self.left = right.astype(jnp.bfloat16), left.astype(jnp.bfloat16)
        return self.right, self.left

    def result(self):
        total = self.block(0) + self.right.astype(jnp.float32) + self.left.astype(jnp.float32)
        return total.astype(jnp.bfloat16)


def slot_table(index, slots):
    count = index.shape[0]
    hit = index[None, :] == jnp.arange(slots, dtype=jnp.int32)[:, None]
    return jnp.min(jnp.where(hit, jnp.arange(count, dtype=jnp.int32)[None, :], count), axis=1)


def with_zero(blocks):
    return jnp.concatenate([blocks, jnp.zeros((1,) + blocks.shape[1:], blocks.dtype)], axis=0)


def columns_of(lhs, weights, place, first, depth):
    strip = jnp.concatenate(
        [
            jnp.concatenate([weights[place(first + n, m)] for n in range(2)], axis=1)
            for m in range(depth)
        ],
        axis=0,
    )
    return jnp.dot(lhs, strip, preferred_element_type=jnp.float32)


def columns_of_turned(lhs, weights, place, first, depth):
    strip = jnp.concatenate(
        [
            jnp.concatenate([weights[place(first + n, m)] for m in range(depth)], axis=1)
            for n in range(2)
        ],
        axis=0,
    )
    return lax.dot_general(
        lhs, strip, (((1,), (1,)), ((), ())), preferred_element_type=jnp.float32
    )


def hidden_kernel(dim_blocks, offset, gate_at, up_at, x, gate_w, up_w, hidden, act, slope):
    first = (offset + pl.program_id(0)) * 2

    def strip(at, w):
        return columns_of(x[...], w, lambda n, m: at[n * dim_blocks + m], first, dim_blocks)

    gate = strip(gate_at, gate_w)
    up = strip(up_at, up_w)
    sig = jax.nn.sigmoid(gate)
    activated = gate * sig
    hidden[...] = (activated * up).astype(jnp.bfloat16)
    act[...] = activated
    slope[...] = up * sig * (1.0 + gate * (1.0 - sig))


def grads_kernel(dim_blocks, offset, down_at, g, down_w, act, slope, gate_grad, up_grad):
    first = (offset + pl.program_id(0)) * 2
    hidden_grad = columns_of_turned(
        g[...], down_w, lambda n, m: down_at[n * dim_blocks + m], first, dim_blocks
    )
    gate_grad[...] = (hidden_grad * slope[...]).astype(jnp.bfloat16)
    up_grad[...] = (hidden_grad * act[...]).astype(jnp.bfloat16)


def split_rows(value, near, far):
    rows = near.shape[0]
    near[...] = value[:rows]
    far[...] = value[rows:].astype(far.dtype)


def output_kernel(dim_blocks, columns, offset, down_at, hidden, down_w, near, far):
    first = (offset + pl.program_id(0)) * 2
    value = columns_of(
        hidden[...], down_w, lambda n, m: down_at[m * dim_blocks + n], first, columns
    )
    split_rows(value, near, far)


def input_grad_kernel(
    dim_blocks, columns, offset, gate_at, up_at, gate_grad, up_grad, gate_w, up_w, near, far
):
    first = (offset + pl.program_id(0)) * 2

    def strip(lhs, at, w):
        return columns_of_turned(
            lhs[...], w, lambda n, m: at[m * dim_blocks + n], first, columns
        )

    split_rows(strip(gate_grad, gate_at, gate_w) + strip(up_grad, up_at, up_w), near, far)


def whole_spec(array):
    zeros = (0,) * len(array.shape)
    return pl.BlockSpec(array.shape, lambda i: zeros, pipeline_mode=pl.Buffered(1))


def room(arrays, spare):
    held = sum(a.dtype.itemsize * a.size for a in arrays)
    return pltpu.CompilerParams(vmem_limit_bytes=held + spare * 2**20)


class Strips:
    def __init__(self, kernel, total, block_outs, flops):
        self.kernel, self.total, self.block_outs, self.flops = kernel, total, block_outs, flops
        self.outs = []

    def run(self, inputs, specs, strips, events=(), half=None):
        first, end = strips
        count = end - first
        parts = 1 if half is None else 2

        def strip_spec(array):
            return pl.BlockSpec(
                (array.shape[0] // parts, 2 * 128), lambda i: (half or 0, first + i)
            )

        in_specs = [
            strip_spec(array) if spec is None else whole_spec(array) if spec is WHOLE else spec
            for array, spec in zip(inputs, specs)
        ] + [ANY_SPEC] * len(self.outs)
        first_out = len(inputs)
        inputs = [*after_all(inputs[:1], events), *inputs[1:], *self.outs]

        def kernel(*refs):
            outs = refs[len(inputs):]
            self.kernel(first, *refs[:first_out], *outs[:-1])
            outs[-1][...] = jnp.zeros_like(outs[-1])

        *outs, token = pl.pallas_call(
            kernel,
            grid=(count,),
            in_specs=in_specs,
            out_specs=[strip_spec(out) for out in self.block_outs]
            + [pl.BlockSpec((8, 128), lambda i: (0, 0))],
            out_shape=list(self.block_outs) + [jax.ShapeDtypeStruct((8, 128), jnp.int32)],
            input_output_aliases={first_out + i: i for i in range(len(self.outs))},
            compiler_params=room(
                [array for array, spec in zip(inputs, specs) if spec is WHOLE], 12
            ),
            cost_estimate=pl.CostEstimate(
                flops=2 * self.flops * count // (self.total * parts), bytes_accessed=8 * 2**20,
                transcendentals=0,
            ),
        )(*inputs)
        self.outs = outs
        return (token,)


def block_grads(model, hidden, index, dim_blocks, model_first, arrived, scale):
    count = index.shape[0]
    rows = model[0].shape[0]
    b = 128
    group = max(d for d in range(1, 13) if count % d == 0)
    extra = [] if arrived is None else [arrived]

    def kernel(at, *refs):
        model_refs, hidden_ref, rest = refs[:len(model)], refs[len(model)], refs[len(model) + 1:]
        out = rest[-1]
        base = pl.program_id(0) * group
        for i in range(group):
            slot = at[base + i]
            model_at = pl.ds(pl.multiple_of(slot % dim_blocks * b, b), b)
            hidden_at = pl.ds(pl.multiple_of(slot // dim_blocks * b, b), b)
            value = None
            for part, ref in enumerate(model_refs):
                pair = (ref[:, model_at], hidden_ref[pl.ds(part * rows, rows), hidden_at])
                term = lax.dot_general(
                    *(pair if model_first else pair[::-1]),
                    (((0,), (0,)), ((), ())),
                    preferred_element_type=jnp.float32,
                )
                value = term if value is None else value + term
            if arrived is not None:
                value = (value + rest[0][i].astype(jnp.float32)) * scale
            out[i] = value.astype(out.dtype)

    spec = pl.BlockSpec((group, b, b), lambda i: (i, 0, 0))
    whole = [*model, hidden]
    dtype = jnp.bfloat16 if arrived is None else jnp.float32
    return pl.pallas_call(
        kernel,
        grid=(count // group,),
        in_specs=[SMEM_SPEC] + [whole_spec(a) for a in whole] + [spec] * len(extra),
        out_specs=spec,
        out_shape=jax.ShapeDtypeStruct((count, b, b), dtype),
        compiler_params=room(whole, 10),
        cost_estimate=pl.CostEstimate(
            flops=8 * count * rows * len(model) * b * b, bytes_accessed=8 * 2**20, transcendentals=0
        ),
    )(index, *whole, *extra)


def body(
    tokens_in, grad_out, gate_blocks, up_blocks, down_blocks, gate_index, up_index, down_index
):
    block_size = gate_blocks.shape[1]
    model_width = tokens_in.shape[1]
    dim_blocks = model_width // block_size
    owners = lax.axis_size("tensor")
    columns = FF // (block_size * owners)
    width = columns * block_size
    token_count = tokens_in.shape[0] * owners
    count = gate_blocks.shape[0]
    slots = columns * dim_blocks

    steps = owners // 2
    unit = 2 * token_count * model_width * width
    narrow = jax.ShapeDtypeStruct((token_count, width), jnp.bfloat16)
    wide = jax.ShapeDtypeStruct((token_count, width), jnp.float32)
    held_rows = tokens_in.shape[0]
    totals = [
        jax.ShapeDtypeStruct((token_count - held_rows, model_width), jnp.float32),
        jax.ShapeDtypeStruct((held_rows, model_width), jnp.bfloat16),
    ]

    assert steps % 4 == 0

    def several(chain, quarters, events=()):
        for _ in range(steps * quarters // 4):
            events = chain.step(events)
        return tuple(events)

    hidden_strips = Strips(
        functools.partial(hidden_kernel, dim_blocks), columns // 2, [narrow, wide, wide], 2 * unit
    )
    out_strips = Strips(
        functools.partial(output_kernel, dim_blocks, columns), dim_blocks // 2, totals, unit
    )
    grads_strips = Strips(
        functools.partial(grads_kernel, dim_blocks), columns // 2, [narrow, narrow], unit
    )
    in_strips = Strips(
        functools.partial(input_grad_kernel, dim_blocks, columns), dim_blocks // 2, totals, 2 * unit
    )
    hidden_all, model_all = columns // 2, dim_blocks // 2

    x_ring, g_ring = Gather(tokens_in, owners), Gather(grad_out, owners)
    events = several(x_ring, 1)
    gate_at, up_at = slot_table(gate_index, slots), slot_table(up_index, slots)
    gate_w = with_zero(gate_blocks)
    events = several(x_ring, 1, events + (gate_at, up_at, gate_w))
    (up_w,) = after_all([with_zero(up_blocks)], events[:0])
    x_low = x_ring.first_rows(events + (up_w,))

    def hidden_run(x, strips, events, half):
        return hidden_strips.run(
            [gate_at, up_at, x, gate_w, up_w], [SMEM_SPEC] * 2 + [WHOLE] * 3, strips, events, half
        )

    events = several(x_ring, 1, events) + hidden_run(x_low, (0, hidden_all // 2), events, 0)
    down_at, down_w = slot_table(down_index, slots), with_zero(down_blocks)
    events = (
        several(x_ring, 1, events)
        + several(g_ring, 1, events)
        + hidden_run(x_low, (hidden_all // 2, hidden_all), events, 0)
        + (down_at, down_w)
    )
    x_high = x_ring.last_rows(events)

    events = several(g_ring, 1, events) + hidden_run(x_high, (0, hidden_all), events, 1)
    hidden, act, slope = hidden_strips.outs
    events = several(g_ring, 1, events) + out_strips.run(
        [down_at, hidden, down_w], [SMEM_SPEC] + [WHOLE] * 2, (0, model_all), events
    )

    out_ring = Scatter(*out_strips.outs, owners)
    events = several(g_ring, 1, events) + several(out_ring, 1)
    g = g_ring.all_rows(events)

    def in_run(strips, events):
        return in_strips.run(
            [gate_at, up_at, *grads_strips.outs, gate_w, up_w], [SMEM_SPEC] * 2 + [WHOLE] * 4,
            strips, events,
        )

    events = several(out_ring, 1, events) + grads_strips.run(
        [down_at, g, down_w, act, slope], [SMEM_SPEC] + [WHOLE] * 2 + [None] * 2,
        (0, hidden_all), events,
    )
    events = several(out_ring, 1, events) + in_run((0, model_all // 2), events)
    events = several(out_ring, 1, events) + in_run((model_all // 2, model_all), events)
    output = out_ring.result()
    gate_grad, up_grad = grads_strips.outs

    in_ring = Scatter(*in_strips.outs, owners)
    pairs = lax.axis_size("dp")
    share = count // pairs
    me = lax.axis_index("dp")
    scale = 1.0 / float(token_count * pairs) ** 0.5
    work = (
        ((g,), hidden, down_index, False),
        ((x_low, x_high), gate_grad, gate_index, True),
        ((x_low, x_high), up_grad, up_index, True),
    )

    def theirs(i, events):
        model, hidden, index, model_first = work[i]
        (held,) = after_all([lax.dynamic_slice(index, ((1 - me) * share,), (share,))], events)
        return block_grads(model, hidden, held, dim_blocks, model_first, None, None)

    def mine(i, arrived, events):
        model, hidden, index, model_first = work[i]
        (held,) = after_all([lax.dynamic_slice(index, (me * share,), (share,))], events)
        return block_grads(model, hidden, held, dim_blocks, model_first, arrived, scale)

    def swap(sent):
        return lax.ppermute(sent, "dp", [(0, 1), (1, 0)])

    sent = theirs(0, events)
    events = several(in_ring, 1, events) + (sent,)
    down_arrived = swap(sent)
    sent = [theirs(1, events), theirs(2, events)]
    events = several(in_ring, 1, events) + (*sent, down_arrived)
    gate_arrived, up_arrived = swap(sent[0]), swap(sent[1])
    down_sum = mine(0, down_arrived, events)
    events = several(in_ring, 1, events) + (down_sum[:1, :8], gate_arrived, up_arrived)
    gate_sum = mine(1, gate_arrived, events)
    up_sum = mine(2, up_arrived, events)
    several(in_ring, 1, events)
    input_grad = in_ring.result()
    return output, input_grad, gate_sum, up_sum, down_sum


def solution(mesh):
    rows = P(("group", "tensor", "dp"), None)
    owned = P("tensor", None, None)
    grads = P(("group", "tensor", "dp"), None, None)
    return jax.shard_map(
        body,
        mesh=mesh,
        in_specs=(rows, rows, owned, owned, owned, P("tensor"), P("tensor"), P("tensor")),
        out_specs=(rows, rows, grads, grads, grads),
        check_vma=False,
    )
```

```python
import functools

import jax
import jax.numpy as jnp
from jax import lax
from jax.experimental import pallas as pl
from jax.experimental.pallas import tpu as pltpu
from jax.sharding import PartitionSpec as P

FF = 12288

SMEM_SPEC = pl.BlockSpec(memory_space=pltpu.SMEM)
WHOLE = "whole"
ANY_SPEC = pl.BlockSpec(memory_space=pl.ANY)


def ring_order(size):
    return list(range(0, size, 2)) + list(range(1, size, 2))[::-1]


def ring_shifts(size):
    order = ring_order(size)
    ahead = [(order[i], order[(i + 1) % size]) for i in range(size)]
    back = [(b, a) for a, b in ahead]

    def to_right(value):
        return lax.ppermute(value, "tensor", ahead)

    def to_left(value):
        return lax.ppermute(value, "tensor", back)

    return to_right, to_left


def after_all(values, events):
    values = tuple(values)
    return lax.optimization_barrier(values + tuple(events))[:len(values)] if events else values


class Gather:
    def __init__(self, rows, size):
        self.to_right, self.to_left = ring_shifts(size)
        self.half = rows.shape[0] // 2
        self.last = size // 2 - 1
        self.blocks = [rows]
        self.from_left = self.from_right = rows
        self.taken = 0

    def step(self, events=()):
        left, right = after_all((self.from_left, self.from_right), events)
        if self.taken == self.last:
            left, right = left[:self.half], right[self.half:]
        self.from_left, self.from_right = self.to_right(left), self.to_left(right)
        self.blocks += [self.from_left, self.from_right]
        self.taken += 1
        return self.from_left, self.from_right

    def first_rows(self, events):
        return jnp.concatenate(after_all(self.blocks[:self.last + 1], events), axis=0)

    def all_rows(self, events):
        return jnp.concatenate(after_all(self.blocks, events), axis=0)

    def last_rows(self, events):
        return jnp.concatenate(after_all(self.blocks[self.last + 1:], events), axis=0)


class Scatter:
    def __init__(self, near, far, size):
        self.to_right, self.to_left = ring_shifts(size)
        self.near = near
        self.rows = far.shape[0]
        self.half = self.rows // 2
        self.distance = size // 2
        self.right, self.left = far[:self.half], far[self.half:]

    def block(self, place):
        return self.near[place * self.rows:(place + 1) * self.rows]

    def step(self, events=()):
        right, left = after_all((self.right, self.left), events)
        right, left = self.to_right(right), self.to_left(left)
        self.distance -= 1
        self.right, self.left = right, left
        if self.distance > 0:
            if right.shape[0] == self.half:
                none = jnp.zeros_like(right)
                right = jnp.concatenate([right, none], axis=0)
                left = jnp.concatenate([none, left], axis=0)
            right = right.astype(jnp.float32) + self.block(2 * self.distance)
            left = left.astype(jnp.float32) + self.block(2 * self.distance - 1)
            self.right, self.left = right.astype(jnp.bfloat16), left.astype(jnp.bfloat16)
        return self.right, self.left

    def result(self):
        total = self.block(0) + self.right.astype(jnp.float32) + self.left.astype(jnp.float32)
        return total.astype(jnp.bfloat16)


def slot_table(index, slots):
    count = index.shape[0]
    hit = index[None, :] == jnp.arange(slots, dtype=jnp.int32)[:, None]
    return jnp.min(jnp.where(hit, jnp.arange(count, dtype=jnp.int32)[None, :], count), axis=1)


def with_zero(blocks):
    return jnp.concatenate([blocks, jnp.zeros((1,) + blocks.shape[1:], blocks.dtype)], axis=0)


def columns_of(lhs, weights, place, first, depth):
    strip = jnp.concatenate(
        [
            jnp.concatenate([weights[place(first + n, m)] for n in range(2)], axis=1)
            for m in range(depth)
        ],
        axis=0,
    )
    return jnp.dot(lhs, strip, preferred_element_type=jnp.float32)


def columns_of_turned(lhs, weights, place, first, depth):
    strip = jnp.concatenate(
        [
            jnp.concatenate([weights[place(first + n, m)] for m in range(depth)], axis=1)
            for n in range(2)
        ],
        axis=0,
    )
    return lax.dot_general(
        lhs, strip, (((1,), (1,)), ((), ())), preferred_element_type=jnp.float32
    )


def hidden_kernel(dim_blocks, offset, gate_at, up_at, x, gate_w, up_w, hidden, act, slope):
    first = (offset + pl.program_id(0)) * 2

    def strip(at, w):
        return columns_of(x[...], w, lambda n, m: at[n * dim_blocks + m], first, dim_blocks)

    gate = strip(gate_at, gate_w)
    up = strip(up_at, up_w)
    sig = jax.nn.sigmoid(gate)
    activated = gate * sig
    hidden[...] = (activated * up).astype(jnp.bfloat16)
    act[...] = activated
    slope[...] = up * sig * (1.0 + gate * (1.0 - sig))


def grads_kernel(dim_blocks, offset, down_at, g, down_w, act, slope, gate_grad, up_grad):
    first = (offset + pl.program_id(0)) * 2
    hidden_grad = columns_of_turned(
        g[...], down_w, lambda n, m: down_at[n * dim_blocks + m], first, dim_blocks
    )
    gate_grad[...] = (hidden_grad * slope[...]).astype(jnp.bfloat16)
    up_grad[...] = (hidden_grad * act[...]).astype(jnp.bfloat16)


def split_rows(value, near, far):
    rows = near.shape[0]
    near[...] = value[:rows]
    far[...] = value[rows:].astype(far.dtype)


def output_kernel(dim_blocks, columns, offset, down_at, hidden, down_w, near, far):
    first = (offset + pl.program_id(0)) * 2
    value = columns_of(
        hidden[...], down_w, lambda n, m: down_at[m * dim_blocks + n], first, columns
    )
    split_rows(value, near, far)


def input_grad_kernel(
    dim_blocks, columns, offset, gate_at, up_at, gate_grad, up_grad, gate_w, up_w, near, far
):
    first = (offset + pl.program_id(0)) * 2

    def strip(lhs, at, w):
        return columns_of_turned(
            lhs[...], w, lambda n, m: at[m * dim_blocks + n], first, columns
        )

    split_rows(strip(gate_grad, gate_at, gate_w) + strip(up_grad, up_at, up_w), near, far)


def whole_spec(array):
    zeros = (0,) * len(array.shape)
    return pl.BlockSpec(array.shape, lambda i: zeros, pipeline_mode=pl.Buffered(1))


def room(arrays, spare):
    held = sum(a.dtype.itemsize * a.size for a in arrays)
    return pltpu.CompilerParams(vmem_limit_bytes=held + spare * 2**20)


class Strips:
    def __init__(self, kernel, total, block_outs, flops):
        self.kernel, self.total, self.block_outs, self.flops = kernel, total, block_outs, flops
        self.outs = []

    def run(self, inputs, specs, strips, events=(), half=None):
        first, end = strips
        count = end - first
        parts = 1 if half is None else 2

        def strip_spec(array):
            return pl.BlockSpec(
                (array.shape[0] // parts, 2 * 128), lambda i: (half or 0, first + i)
            )

        in_specs = [
            strip_spec(array) if spec is None else whole_spec(array) if spec is WHOLE else spec
            for array, spec in zip(inputs, specs)
        ] + [ANY_SPEC] * len(self.outs)
        first_out = len(inputs)
        inputs = [*after_all(inputs[:1], events), *inputs[1:], *self.outs]

        def kernel(*refs):
            outs = refs[len(inputs):]
            self.kernel(first, *refs[:first_out], *outs[:-1])
            outs[-1][...] = jnp.zeros_like(outs[-1])

        *outs, token = pl.pallas_call(
            kernel,
            grid=(count,),
            in_specs=in_specs,
            out_specs=[strip_spec(out) for out in self.block_outs]
            + [pl.BlockSpec((8, 128), lambda i: (0, 0))],
            out_shape=list(self.block_outs) + [jax.ShapeDtypeStruct((8, 128), jnp.int32)],
            input_output_aliases={first_out + i: i for i in range(len(self.outs))},
            compiler_params=room(
                [array for array, spec in zip(inputs, specs) if spec is WHOLE], 12
            ),
            cost_estimate=pl.CostEstimate(
                flops=2 * self.flops * count // (self.total * parts), bytes_accessed=8 * 2**20,
                transcendentals=0,
            ),
        )(*inputs)
        self.outs = outs
        return (token,)


def block_grads(model, hidden, index, dim_blocks, model_first, arrived, scale):
    count = index.shape[0]
    rows = model[0].shape[0]
    b = 128
    group = max(d for d in range(1, 13) if count % d == 0)
    extra = [] if arrived is None else [arrived]

    def kernel(at, *refs):
        model_refs, hidden_ref, rest = refs[:len(model)], refs[len(model)], refs[len(model) + 1:]
        out = rest[-1]
        base = pl.program_id(0) * group
        for i in range(group):
            slot = at[base + i]
            model_at = pl.ds(pl.multiple_of(slot % dim_blocks * b, b), b)
            hidden_at = pl.ds(pl.multiple_of(slot // dim_blocks * b, b), b)
            value = None
            for part, ref in enumerate(model_refs):
                pair = (ref[:, model_at], hidden_ref[pl.ds(part * rows, rows), hidden_at])
                term = lax.dot_general(
                    *(pair if model_first else pair[::-1]),
                    (((0,), (0,)), ((), ())),
                    preferred_element_type=jnp.float32,
                )
                value = term if value is None else value + term
            if arrived is not None:
                value = (value + rest[0][i].astype(jnp.float32)) * scale
            out[i] = value.astype(out.dtype)

    spec = pl.BlockSpec((group, b, b), lambda i: (i, 0, 0))
    whole = [*model, hidden]
    dtype = jnp.bfloat16 if arrived is None else jnp.float32
    return pl.pallas_call(
        kernel,
        grid=(count // group,),
        in_specs=[SMEM_SPEC] + [whole_spec(a) for a in whole] + [spec] * len(extra),
        out_specs=spec,
        out_shape=jax.ShapeDtypeStruct((count, b, b), dtype),
        compiler_params=room(whole, 10),
        cost_estimate=pl.CostEstimate(
            flops=8 * count * rows * len(model) * b * b, bytes_accessed=8 * 2**20, transcendentals=0
        ),
    )(index, *whole, *extra)


def body(
    tokens_in, grad_out, gate_blocks, up_blocks, down_blocks, gate_index, up_index, down_index
):
    block_size = gate_blocks.shape[1]
    model_width = tokens_in.shape[1]
    dim_blocks = model_width // block_size
    owners = lax.axis_size("tensor")
    columns = FF // (block_size * owners)
    width = columns * block_size
    token_count = tokens_in.shape[0] * owners
    count = gate_blocks.shape[0]
    slots = columns * dim_blocks

    steps = owners // 2
    unit = 2 * token_count * model_width * width
    narrow = jax.ShapeDtypeStruct((token_count, width), jnp.bfloat16)
    wide = jax.ShapeDtypeStruct((token_count, width), jnp.float32)
    held_rows = tokens_in.shape[0]
    totals = [
        jax.ShapeDtypeStruct((token_count - held_rows, model_width), jnp.float32),
        jax.ShapeDtypeStruct((held_rows, model_width), jnp.bfloat16),
    ]

    assert steps % 4 == 0

    def several(chain, quarters, events=()):
        for _ in range(steps * quarters // 4):
            events = chain.step(events)
        return tuple(events)

    hidden_strips = Strips(
        functools.partial(hidden_kernel, dim_blocks), columns // 2, [narrow, wide, wide], 2 * unit
    )
    out_strips = Strips(
        functools.partial(output_kernel, dim_blocks, columns), dim_blocks // 2, totals, unit
    )
    grads_strips = Strips(
        functools.partial(grads_kernel, dim_blocks), columns // 2, [narrow, narrow], unit
    )
    in_strips = Strips(
        functools.partial(input_grad_kernel, dim_blocks, columns), dim_blocks // 2, totals, 2 * unit
    )
    hidden_all, model_all = columns // 2, dim_blocks // 2

    x_ring, g_ring = Gather(tokens_in, owners), Gather(grad_out, owners)
    events = several(x_ring, 1)
    gate_at, up_at = slot_table(gate_index, slots), slot_table(up_index, slots)
    gate_w = with_zero(gate_blocks)
    events = several(x_ring, 1, events + (gate_at, up_at, gate_w))
    (up_w,) = after_all([with_zero(up_blocks)], events[:0])
    x_low = x_ring.first_rows(events + (up_w,))

    def hidden_run(x, strips, events, half):
        return hidden_strips.run(
            [gate_at, up_at, x, gate_w, up_w], [SMEM_SPEC] * 2 + [WHOLE] * 3, strips, events, half
        )

    events = several(x_ring, 1, events) + hidden_run(x_low, (0, hidden_all // 2), events, 0)
    down_at, down_w = slot_table(down_index, slots), with_zero(down_blocks)
    events = (
        several(x_ring, 1, events)
        + several(g_ring, 1, events)
        + hidden_run(x_low, (hidden_all // 2, hidden_all), events, 0)
        + (down_at, down_w)
    )
    x_high = x_ring.last_rows(events)

    events = several(g_ring, 1, events) + hidden_run(x_high, (0, hidden_all), events, 1)
    hidden, act, slope = hidden_strips.outs
    events = several(g_ring, 1, events) + out_strips.run(
        [down_at, hidden, down_w], [SMEM_SPEC] + [WHOLE] * 2, (0, model_all), events
    )

    out_ring = Scatter(*out_strips.outs, owners)
    events = several(g_ring, 1, events)
    g = g_ring.all_rows(events)

    def in_run(strips, events):
        return in_strips.run(
            [gate_at, up_at, *grads_strips.outs, gate_w, up_w], [SMEM_SPEC] * 2 + [WHOLE] * 4,
            strips, events,
        )

    def grads_run(strips, events):
        return grads_strips.run(
            [down_at, g, down_w, act, slope], [SMEM_SPEC] + [WHOLE] * 2 + [None] * 2,
            strips, events,
        )

    middle, quarter = hidden_all // 2, model_all // 4
    events = several(out_ring, 1, events) + grads_run((0, middle), events)
    token = grads_run((middle, hidden_all), events)
    events = several(out_ring, 1, events) + in_run((0, quarter), token)
    events = several(out_ring, 1, events) + in_run((quarter, 3 * quarter), events)
    token = in_run((3 * quarter, model_all), events)
    last_out = several(out_ring, 1, events)
    output = out_ring.result()
    gate_grad, up_grad = grads_strips.outs

    in_ring = Scatter(*in_strips.outs, owners)
    pairs = lax.axis_size("dp")
    share = count // pairs
    me = lax.axis_index("dp")
    scale = 1.0 / float(token_count * pairs) ** 0.5
    work = (
        ((g,), hidden, down_index, False),
        ((x_low, x_high), gate_grad, gate_index, True),
        ((x_low, x_high), up_grad, up_index, True),
    )

    def theirs(i, events):
        model, hidden, index, model_first = work[i]
        (held,) = after_all([lax.dynamic_slice(index, ((1 - me) * share,), (share,))], events)
        return block_grads(model, hidden, held, dim_blocks, model_first, None, None)

    def mine(i, arrived, events):
        model, hidden, index, model_first = work[i]
        (held,) = after_all([lax.dynamic_slice(index, (me * share,), (share,))], events)
        return block_grads(model, hidden, held, dim_blocks, model_first, arrived, scale)

    def swap(sent):
        return lax.ppermute(sent, "dp", [(0, 1), (1, 0)])

    sent = theirs(0, token)
    events = several(in_ring, 1) + last_out + (sent,)
    down_arrived = swap(sent)
    sent = [theirs(1, events), theirs(2, events)]
    events = several(in_ring, 1, events) + (*sent, down_arrived)
    gate_arrived, up_arrived = swap(sent[0]), swap(sent[1])
    down_sum = mine(0, down_arrived, events)
    events = several(in_ring, 1, events) + (down_sum[:1, :8], gate_arrived, up_arrived)
    gate_sum = mine(1, gate_arrived, events)
    up_sum = mine(2, up_arrived, events)
    several(in_ring, 1, events)
    input_grad = in_ring.result()
    return output, input_grad, gate_sum, up_sum, down_sum


def solution(mesh):
    rows = P(("group", "tensor", "dp"), None)
    owned = P("tensor", None, None)
    grads = P(("group", "tensor", "dp"), None, None)
    return jax.shard_map(
        body,
        mesh=mesh,
        in_specs=(rows, rows, owned, owned, owned, P("tensor"), P("tensor"), P("tensor")),
        out_specs=(rows, rows, grads, grads, grads),
        check_vma=False,
    )
```

```python
import functools

import jax
import jax.numpy as jnp
from jax import lax
from jax.experimental import pallas as pl
from jax.experimental.pallas import tpu as pltpu
from jax.sharding import PartitionSpec as P

FF = 12288

SMEM_SPEC = pl.BlockSpec(memory_space=pltpu.SMEM)
WHOLE = "whole"
ANY_SPEC = pl.BlockSpec(memory_space=pl.ANY)


def ring_order(size):
    return list(range(0, size, 2)) + list(range(1, size, 2))[::-1]


def ring_shifts(size):
    order = ring_order(size)
    ahead = [(order[i], order[(i + 1) % size]) for i in range(size)]
    back = [(b, a) for a, b in ahead]

    def to_right(value):
        return lax.ppermute(value, "tensor", ahead)

    def to_left(value):
        return lax.ppermute(value, "tensor", back)

    return to_right, to_left


def after_all(values, events):
    values = tuple(values)
    return lax.optimization_barrier(values + tuple(events))[:len(values)] if events else values


class Gather:
    def __init__(self, rows, size):
        self.to_right, self.to_left = ring_shifts(size)
        self.half = rows.shape[0] // 2
        self.last = size // 2 - 1
        self.blocks = [rows]
        self.from_left = self.from_right = rows
        self.taken = 0

    def step(self, events=()):
        left, right = after_all((self.from_left, self.from_right), events)
        if self.taken == self.last:
            left, right = left[:self.half], right[self.half:]
        self.from_left, self.from_right = self.to_right(left), self.to_left(right)
        self.blocks += [self.from_left, self.from_right]
        self.taken += 1
        return self.from_left, self.from_right

    def first_rows(self, events):
        return jnp.concatenate(after_all(self.blocks[:self.last + 1], events), axis=0)

    def all_rows(self, events):
        return jnp.concatenate(after_all(self.blocks, events), axis=0)

    def last_rows(self, events):
        return jnp.concatenate(after_all(self.blocks[self.last + 1:], events), axis=0)


class Scatter:
    def __init__(self, near, far, size):
        self.to_right, self.to_left = ring_shifts(size)
        self.near = near
        self.rows = far.shape[0]
        self.half = self.rows // 2
        self.distance = size // 2
        self.right, self.left = far[:self.half], far[self.half:]

    def block(self, place):
        return self.near[place * self.rows:(place + 1) * self.rows]

    def step(self, events=()):
        right, left = after_all((self.right, self.left), events)
        right, left = self.to_right(right), self.to_left(left)
        self.distance -= 1
        self.right, self.left = right, left
        if self.distance > 0:
            if right.shape[0] == self.half:
                none = jnp.zeros_like(right)
                right = jnp.concatenate([right, none], axis=0)
                left = jnp.concatenate([none, left], axis=0)
            right = right.astype(jnp.float32) + self.block(2 * self.distance)
            left = left.astype(jnp.float32) + self.block(2 * self.distance - 1)
            self.right, self.left = right.astype(jnp.bfloat16), left.astype(jnp.bfloat16)
        return self.right, self.left

    def result(self):
        total = self.block(0) + self.right.astype(jnp.float32) + self.left.astype(jnp.float32)
        return total.astype(jnp.bfloat16)


def slot_table(index, slots):
    count = index.shape[0]
    hit = index[None, :] == jnp.arange(slots, dtype=jnp.int32)[:, None]
    return jnp.min(jnp.where(hit, jnp.arange(count, dtype=jnp.int32)[None, :], count), axis=1)


def with_zero(blocks):
    return jnp.concatenate([blocks, jnp.zeros((1,) + blocks.shape[1:], blocks.dtype)], axis=0)


def columns_of(lhs, weights, place, first, depth):
    strip = jnp.concatenate(
        [
            jnp.concatenate([weights[place(first + n, m)] for n in range(2)], axis=1)
            for m in range(depth)
        ],
        axis=0,
    )
    return jnp.dot(lhs, strip, preferred_element_type=jnp.float32)


def columns_of_turned(lhs, weights, place, first, depth):
    strip = jnp.concatenate(
        [
            jnp.concatenate([weights[place(first + n, m)] for m in range(depth)], axis=1)
            for n in range(2)
        ],
        axis=0,
    )
    return lax.dot_general(
        lhs, strip, (((1,), (1,)), ((), ())), preferred_element_type=jnp.float32
    )


def hidden_kernel(dim_blocks, offset, gate_at, up_at, x, gate_w, up_w, hidden, act, slope):
    first = (offset + pl.program_id(0)) * 2

    def strip(at, w):
        return columns_of(x[...], w, lambda n, m: at[n * dim_blocks + m], first, dim_blocks)

    gate = strip(gate_at, gate_w)
    up = strip(up_at, up_w)
    sig = jax.nn.sigmoid(gate)
    activated = gate * sig
    hidden[...] = (activated * up).astype(jnp.bfloat16)
    act[...] = activated
    slope[...] = up * sig * (1.0 + gate * (1.0 - sig))


def grads_kernel(dim_blocks, offset, down_at, g, down_w, act, slope, gate_grad, up_grad):
    first = (offset + pl.program_id(0)) * 2
    hidden_grad = columns_of_turned(
        g[...], down_w, lambda n, m: down_at[n * dim_blocks + m], first, dim_blocks
    )
    gate_grad[...] = (hidden_grad * slope[...]).astype(jnp.bfloat16)
    up_grad[...] = (hidden_grad * act[...]).astype(jnp.bfloat16)


def split_rows(value, near, far):
    rows = near.shape[0]
    near[...] = value[:rows]
    far[...] = value[rows:].astype(far.dtype)


def output_kernel(dim_blocks, columns, offset, down_at, hidden, down_w, near, far):
    first = (offset + pl.program_id(0)) * 2
    value = columns_of(
        hidden[...], down_w, lambda n, m: down_at[m * dim_blocks + n], first, columns
    )
    split_rows(value, near, far)


def input_grad_kernel(
    dim_blocks, columns, offset, gate_at, up_at, gate_grad, up_grad, gate_w, up_w, near, far
):
    first = (offset + pl.program_id(0)) * 2

    def strip(lhs, at, w):
        return columns_of_turned(
            lhs[...], w, lambda n, m: at[m * dim_blocks + n], first, columns
        )

    split_rows(strip(gate_grad, gate_at, gate_w) + strip(up_grad, up_at, up_w), near, far)


def whole_spec(array):
    zeros = (0,) * len(array.shape)
    return pl.BlockSpec(array.shape, lambda i: zeros, pipeline_mode=pl.Buffered(1))


def room(arrays, spare):
    held = sum(a.dtype.itemsize * a.size for a in arrays)
    return pltpu.CompilerParams(vmem_limit_bytes=held + spare * 2**20)


class Strips:
    def __init__(self, kernel, total, block_outs, flops):
        self.kernel, self.total, self.block_outs, self.flops = kernel, total, block_outs, flops
        self.outs = []

    def run(self, inputs, specs, strips, events=(), half=None):
        first, end = strips
        count = end - first
        parts = 1 if half is None else 2

        def strip_spec(array):
            return pl.BlockSpec(
                (array.shape[0] // parts, 2 * 128), lambda i: (half or 0, first + i)
            )

        in_specs = [
            strip_spec(array) if spec is None else whole_spec(array) if spec is WHOLE else spec
            for array, spec in zip(inputs, specs)
        ] + [ANY_SPEC] * len(self.outs)
        first_out = len(inputs)
        inputs = [*after_all(inputs[:1], events), *inputs[1:], *self.outs]

        def kernel(*refs):
            outs = refs[len(inputs):]
            self.kernel(first, *refs[:first_out], *outs[:-1])
            outs[-1][...] = jnp.zeros_like(outs[-1])

        *outs, token = pl.pallas_call(
            kernel,
            grid=(count,),
            in_specs=in_specs,
            out_specs=[strip_spec(out) for out in self.block_outs]
            + [pl.BlockSpec((8, 128), lambda i: (0, 0))],
            out_shape=list(self.block_outs) + [jax.ShapeDtypeStruct((8, 128), jnp.int32)],
            input_output_aliases={first_out + i: i for i in range(len(self.outs))},
            compiler_params=room(
                [array for array, spec in zip(inputs, specs) if spec is WHOLE], 12
            ),
            cost_estimate=pl.CostEstimate(
                flops=2 * self.flops * count // (self.total * parts), bytes_accessed=8 * 2**20,
                transcendentals=0,
            ),
        )(*inputs)
        self.outs = outs
        return (token,)


def block_grads(model, hidden, index, dim_blocks, model_first, arrived, scale):
    count = index.shape[0]
    rows = model[0].shape[0]
    b = 128
    group = max(d for d in range(1, 13) if count % d == 0)
    extra = [] if arrived is None else [arrived]

    def kernel(at, *refs):
        model_refs, hidden_ref, rest = refs[:len(model)], refs[len(model)], refs[len(model) + 1:]
        out = rest[-1]
        base = pl.program_id(0) * group
        for i in range(group):
            slot = at[base + i]
            model_at = pl.ds(pl.multiple_of(slot % dim_blocks * b, b), b)
            hidden_at = pl.ds(pl.multiple_of(slot // dim_blocks * b, b), b)
            value = None
            for part, ref in enumerate(model_refs):
                pair = (ref[:, model_at], hidden_ref[pl.ds(part * rows, rows), hidden_at])
                term = lax.dot_general(
                    *(pair if model_first else pair[::-1]),
                    (((0,), (0,)), ((), ())),
                    preferred_element_type=jnp.float32,
                )
                value = term if value is None else value + term
            if arrived is not None:
                value = (value + rest[0][i].astype(jnp.float32)) * scale
            out[i] = value.astype(out.dtype)

    spec = pl.BlockSpec((group, b, b), lambda i: (i, 0, 0))
    whole = [*model, hidden]
    dtype = jnp.bfloat16 if arrived is None else jnp.float32
    return pl.pallas_call(
        kernel,
        grid=(count // group,),
        in_specs=[SMEM_SPEC] + [whole_spec(a) for a in whole] + [spec] * len(extra),
        out_specs=spec,
        out_shape=jax.ShapeDtypeStruct((count, b, b), dtype),
        compiler_params=room(whole, 10),
        cost_estimate=pl.CostEstimate(
            flops=8 * count * rows * len(model) * b * b, bytes_accessed=8 * 2**20, transcendentals=0
        ),
    )(index, *whole, *extra)


def body(
    tokens_in, grad_out, gate_blocks, up_blocks, down_blocks, gate_index, up_index, down_index
):
    block_size = gate_blocks.shape[1]
    model_width = tokens_in.shape[1]
    dim_blocks = model_width // block_size
    owners = lax.axis_size("tensor")
    columns = FF // (block_size * owners)
    width = columns * block_size
    token_count = tokens_in.shape[0] * owners
    count = gate_blocks.shape[0]
    slots = columns * dim_blocks

    steps = owners // 2
    unit = 2 * token_count * model_width * width
    narrow = jax.ShapeDtypeStruct((token_count, width), jnp.bfloat16)
    wide = jax.ShapeDtypeStruct((token_count, width), jnp.float32)
    held_rows = tokens_in.shape[0]
    totals = [
        jax.ShapeDtypeStruct((token_count - held_rows, model_width), jnp.float32),
        jax.ShapeDtypeStruct((held_rows, model_width), jnp.bfloat16),
    ]

    assert steps % 4 == 0

    def several(chain, quarters, events=()):
        for _ in range(steps * quarters // 4):
            events = chain.step(events)
        return tuple(events)

    hidden_strips = Strips(
        functools.partial(hidden_kernel, dim_blocks), columns // 2, [narrow, wide, wide], 2 * unit
    )
    out_strips = Strips(
        functools.partial(output_kernel, dim_blocks, columns), dim_blocks // 2, totals, unit
    )
    grads_strips = Strips(
        functools.partial(grads_kernel, dim_blocks), columns // 2, [narrow, narrow], unit
    )
    in_strips = Strips(
        functools.partial(input_grad_kernel, dim_blocks, columns), dim_blocks // 2, totals, 2 * unit
    )
    hidden_all, model_all = columns // 2, dim_blocks // 2

    x_ring, g_ring = Gather(tokens_in, owners), Gather(grad_out, owners)
    events = several(x_ring, 1)
    gate_at, up_at = slot_table(gate_index, slots), slot_table(up_index, slots)
    gate_w = with_zero(gate_blocks)
    events = several(x_ring, 1, events + (gate_at, up_at, gate_w))
    (up_w,) = after_all([with_zero(up_blocks)], events[:0])
    x_low = x_ring.first_rows(events + (up_w,))

    def hidden_run(x, strips, events, half):
        return hidden_strips.run(
            [gate_at, up_at, x, gate_w, up_w], [SMEM_SPEC] * 2 + [WHOLE] * 3, strips, events, half
        )

    events = several(x_ring, 1, events) + hidden_run(x_low, (0, hidden_all // 2), events, 0)
    down_at, down_w = slot_table(down_index, slots), with_zero(down_blocks)
    events = (
        several(x_ring, 1, events)
        + several(g_ring, 1, events)
        + hidden_run(x_low, (hidden_all // 2, hidden_all), events, 0)
        + (down_at, down_w)
    )
    x_high = x_ring.last_rows(events)

    events = several(g_ring, 1, events) + hidden_run(x_high, (0, hidden_all), events, 1)
    hidden, act, slope = hidden_strips.outs
    events = several(g_ring, 1, events) + out_strips.run(
        [down_at, hidden, down_w], [SMEM_SPEC] + [WHOLE] * 2, (0, model_all), events
    )

    out_ring = Scatter(*out_strips.outs, owners)
    events = several(g_ring, 1, events)
    g = g_ring.all_rows(events)

    def in_run(strips, events):
        return in_strips.run(
            [gate_at, up_at, *grads_strips.outs, gate_w, up_w], [SMEM_SPEC] * 2 + [WHOLE] * 4,
            strips, events,
        )

    def grads_run(strips, events):
        return grads_strips.run(
            [down_at, g, down_w, act, slope], [SMEM_SPEC] + [WHOLE] * 2 + [None] * 2,
            strips, events,
        )

    middle, quarter = hidden_all // 2, model_all // 4
    events = several(out_ring, 1, events) + grads_run((0, middle), events)
    token = grads_run((middle, hidden_all), events)
    events = several(out_ring, 1, events) + in_run((0, quarter), token)
    events = several(out_ring, 1, events) + in_run((quarter, 3 * quarter), events)
    token = in_run((3 * quarter, model_all), events)
    last_out = several(out_ring, 1, events)
    output = out_ring.result()
    gate_grad, up_grad = grads_strips.outs

    in_ring = Scatter(*in_strips.outs, owners)
    pairs = lax.axis_size("dp")
    share = count // pairs
    me = lax.axis_index("dp")
    scale = 1.0 / float(token_count * pairs) ** 0.5
    work = (
        ((g,), hidden, down_index, False),
        ((x_low, x_high), gate_grad, gate_index, True),
        ((x_low, x_high), up_grad, up_index, True),
    )

    def theirs(i, events):
        model, hidden, index, model_first = work[i]
        (held,) = after_all([lax.dynamic_slice(index, ((1 - me) * share,), (share,))], events)
        return block_grads(model, hidden, held, dim_blocks, model_first, None, None)

    def mine(i, arrived, events):
        model, hidden, index, model_first = work[i]
        (held,) = after_all([lax.dynamic_slice(index, (me * share,), (share,))], events)
        return block_grads(model, hidden, held, dim_blocks, model_first, arrived, scale)

    def swap(sent):
        return lax.ppermute(sent, "dp", [(0, 1), (1, 0)])

    sent = theirs(0, token + last_out)
    events = several(in_ring, 1) + last_out + (sent,)
    down_arrived = swap(sent)
    sent = [theirs(1, events), theirs(2, events)]
    events = several(in_ring, 1, events) + (*sent, down_arrived)
    gate_arrived, up_arrived = swap(sent[0]), swap(sent[1])
    down_sum = mine(0, down_arrived, events)
    events = several(in_ring, 1, events) + (down_sum[:1, :8], gate_arrived, up_arrived)
    gate_sum = mine(1, gate_arrived, events)
    up_sum = mine(2, up_arrived, events)
    several(in_ring, 1, events)
    input_grad = in_ring.result()
    return output, input_grad, gate_sum, up_sum, down_sum


def solution(mesh):
    rows = P(("group", "tensor", "dp"), None)
    owned = P("tensor", None, None)
    grads = P(("group", "tensor", "dp"), None, None)
    return jax.shard_map(
        body,
        mesh=mesh,
        in_specs=(rows, rows, owned, owned, owned, P("tensor"), P("tensor"), P("tensor")),
        out_specs=(rows, rows, grads, grads, grads),
        check_vma=False,
    )
```
